32 devices in a mesh: grp: 2 (over x), reg: 16 (over z, y, core).
Axes of the slice: x: 2, y: 2, z: 4, core: 2. Of those that a mesh axis runs over, the one named last changes fastest.
Arguments:
- expect_marks: float32 [256, 256, 16, 2], P(('grp', 'reg')), parts along dimension 0, may hold values from -6 to 6
- policy_resp: bfloat16 [256, 256, 2, 128], P(('grp', 'reg')), parts along dimension 0, may hold values from -0.0029296875 to 0.0029296875
- lottery_weight: float32 [256, 256], P('grp'), parts along dimension 0, may hold values from 0 to 1
- lottery_index: int32 [256, 256], P('grp'), parts along dimension 0, may hold values from 0 to 254, as said below
- migration_weight: float32 [256, 4], P('grp'), parts along dimension 0, may hold values from 0.2 to 5
- neighbours: int32 [256, 4], P('grp'), parts along dimension 0, may hold values from 0 to 127, as said below
Outputs:
- jacobian: float32 [256, 2, 2, 128], P(('grp', 'reg')), parts along dimension 0
The draws below stay inside these ranges and needn't reach their ends.
There are 2 independent parts, one for each index of `grp`. The reference program is written for one: setup_inputs(seed, part) draws one part's arguments, and reference() takes and returns one part's arrays. A program takes and returns all parts, laid end to end along the dimension named above; each array names one. Nothing has to cross between parts.
Inputs may be any that keep to these rules, and one draw needn't show every extreme that they name: `lottery_index`: each point's lower bracket lies within 2 points of it; the first point's is 0 and the last point's is 254. `neighbours`: every destination lies within 2 regions of its own region; the first entry of each list is the region itself.
All inputs are finite; a program needn't handle non-finite values.
Results may differ from the reference program's by a relative error of at most 0.0029.
Values sent between devices are 32-bit elements; how exact they have to be, the bound alone decides.
A program may use at most 128 MiB of HBM per device.

```python
import math
import jax
import jax.numpy as jnp
from jax import lax

A = 256
O = 2
I = 2
K = 4
REACH = 2
H = 8
R = 128
T_SIZE = 128
NCK = 16


def draw_lottery_index(key, part):
    key = jax.random.fold_in(key, 17)
    offsets = jax.random.randint(key, (R, A), -2, 3, dtype=jnp.int32)
    points = jnp.arange(A, dtype=jnp.int32)[None, :]
    edges = (points == 0) | (points == A - 1)
    offsets = jnp.where(edges, 0, offsets)
    return jnp.clip(points + offsets, 0, A - 2).astype(jnp.int32)


def draw_neighbours(key, part):
    key = jax.random.fold_in(key, 29)
    offsets = jax.random.randint(key, (R, K - 1), -REACH, REACH + 1, dtype=jnp.int32)
    offsets = jnp.concatenate([jnp.zeros((R, 1), jnp.int32), offsets], axis=1)
    regions = jnp.arange(R, dtype=jnp.int32)[:, None]
    return jnp.clip(regions + offsets, 0, R - 1).astype(jnp.int32)


def level_of(key, shape, split, low, high):
    def one(position, blocks):
        steps = jax.random.uniform(jax.random.fold_in(jax.random.fold_in(key, 6), position), (blocks,), jnp.float32, low / len(split), high / len(split))
        return jnp.repeat(jnp.exp(steps), shape[position] // blocks).reshape((-1,) + (1,) * (len(shape) - position - 1))

    factor_of = one(*split[0])
    for cut in split[1:]:
        factor_of = factor_of * one(*cut)
    return factor_of


def noise(key, shape, spread, reach, split=(), kind=jnp.bfloat16):
    entries = jax.random.normal(key, shape, jnp.float32) * spread
    if len(split) > 0:
        entries = level_of(key, shape, split, -0.22, 0.18) * entries
    return jnp.clip(entries, min=-reach, max=reach).astype(kind)


def setup_inputs(seed: int = 0, part: int = 0) -> dict:
    key_of = jax.random.split(jax.random.key(seed), 7)
    part_keys = jax.random.split(jax.random.fold_in(key_of[6], part), 7)
    return {
        "expect_marks": noise(part_keys[0], (R, A, NCK, O), 1.0, 6.0, ((0, 16),), jnp.float32),
        "policy_resp": noise(part_keys[1], (R, A, I, T_SIZE), (R * A * T_SIZE) ** -0.5, 0.0029296875, ((0, 16),)),
        "lottery_weight": jnp.clip(jax.random.uniform(part_keys[2], (R, A), jnp.float32, 0.0, 1.0), 0.0, 1.0),
        "lottery_index": draw_lottery_index(jax.random.fold_in(jax.random.fold_in(key_of[6], part), 71), part),
        "migration_weight": jnp.clip(jnp.exp(jax.random.uniform(part_keys[4], (R, K), jnp.float32, math.log(0.2), math.log(5.0))), 0.2, 5.0),
        "neighbours": draw_neighbours(jax.random.fold_in(jax.random.fold_in(key_of[6], part), 71), part),
    }


def mix_rows(mix_weights, neighbours, state_field):
    mixed_total = jnp.zeros_like(state_field)
    for column_index in range(neighbours.shape[1]):
        mixed_total = mixed_total + mix_weights[:, column_index][:, None, None] * state_field[neighbours[:, column_index]]
    return mixed_total


def lottery(lottery_weight, lottery_index, mixed_field):
    index_full = jnp.broadcast_to(lottery_index[:, :, None], mixed_field.shape)
    below_side = jnp.take_along_axis(mixed_field, index_full, axis=1)
    above_side = jnp.take_along_axis(mixed_field, index_full + 1, axis=1)
    omega_rows = lottery_weight[:, :, None]
    return omega_rows * below_side + (1.0 - omega_rows) * above_side


def reference(expect_marks, policy_resp, lottery_weight, lottery_index, migration_weight, neighbours):
    mix_weights = migration_weight / jnp.sum(migration_weight, axis=1, keepdims=True)
    state_field = expect_marks.reshape(R, A, NCK * O)
    flat_policy = policy_resp.reshape(R * A, I * T_SIZE)
    news_blocks = []
    for horizon in range(H):
        if horizon > 0:
            state_field = lottery(lottery_weight, lottery_index, mix_rows(mix_weights, neighbours, state_field))
        rounded = state_field.astype(jnp.bfloat16).reshape(R * A, NCK * O)
        news_blocks.append(lax.dot_general(rounded, flat_policy, (((0,), (0,)), ((), ())), preferred_element_type=jnp.float32))
    fake = jnp.stack(news_blocks, axis=0).reshape(H, NCK, O, I, T_SIZE)
    fake = jnp.transpose(fake, (1, 0, 2, 3, 4)).reshape(T_SIZE, O, I, T_SIZE)

    def cumulate(previous, news_row):
        current_row = news_row + jnp.pad(previous[:, :, :-1], ((0, 0), (0, 0), (1, 0)))
        return current_row, current_row

    zero_row = jnp.zeros((O, I, T_SIZE), jnp.float32)
    ignored, jacobian = lax.scan(cumulate, zero_row, fake)
    return jacobian
```

```python
import functools
import jax
import jax.numpy as jnp
from jax import lax
from jax.experimental import pallas as pl
from jax.experimental.pallas import tpu as pltpu
from jax.sharding import PartitionSpec as P

REACH = 2
H = 8
FIRST = 4


def kernel(n, e_ref, pol_hbm, lw_ref, li_ref, mw_ref, nb_ref, out_ref,
           x0, x1, x2, eb, pol, acc, coef, wb, wt, jp, ra, sb, rb,
           psem, hsend, hrecv, asem, bsend, brecv):
    regions, cols, points = e_ref.shape
    length = pol.shape[2] // 2
    chips = n // 2
    d = lax.axis_index("reg")
    par = lax.rem(d, 2)
    chip = lax.div(d, 2)
    sib = d + 1 - 2 * par

    policy_copy = pltpu.make_async_copy(pol_hbm, pol, psem)
    policy_copy.start()

    barrier = pltpu.get_barrier_semaphore()

    def greet(other):
        pl.semaphore_signal(barrier, inc=1, device_id={"reg": other},
                            device_id_type=pl.DeviceIdType.MESH)

    @pl.when(d > 0)
    def _():
        greet(d - 1)

    @pl.when(d < n - 1)
    def _():
        greet(d + 1)

    for off in range(1, chips):
        greet(2 * lax.rem(chip + off, chips) + par)
    ends = jnp.where(d > 0, 1, 0) + jnp.where(d < n - 1, 1, 0)
    pl.semaphore_wait(barrier, ends + (chips - 1))

    def halo(stage, to_left):
        if stage == 0:
            src = e_ref
            buf, width = x0, regions
            lo = 0
        else:
            width = (H - 1 - FIRST) * REACH
            lo = regions if to_left else 2 * regions - width
            src = x2.at[pl.ds(lo, width)]
            buf = x2
        dst = buf.at[pl.ds(2 * regions if to_left else regions - width, width)]
        side = 0 if to_left else 1
        return pltpu.make_async_remote_copy(
            src_ref=src, dst_ref=dst,
            send_sem=hsend.at[stage, side], recv_sem=hrecv.at[stage, side],
            device_id={"reg": d - 1 if to_left else d + 1},
            device_id_type=pl.DeviceIdType.MESH)

    def start_halo(stage):
        @pl.when(d > 0)
        def _():
            halo(stage, True).start()

        @pl.when(d < n - 1)
        def _():
            halo(stage, False).start()

    def wait_halo(stage):
        @pl.when(d > 0)
        def _():
            halo(stage, True).wait_send()
            halo(stage, False).wait_recv()

        @pl.when(d < n - 1)
        def _():
            halo(stage, False).wait_send()
            halo(stage, True).wait_recv()

    start_halo(0)

    mw = mw_ref[...]
    mix = mw / jnp.sum(mw, axis=0, keepdims=True)
    offs = nb_ref[...] - lax.broadcasted_iota(jnp.int32, mw.shape, 1)
    rows = [jnp.sum(jnp.where(offs == o, mix, 0.0), axis=0, keepdims=True)
            for o in range(-REACH, REACH + 1)]
    rows.append(jnp.zeros((8 - len(rows), mw.shape[1]), jnp.float32))
    wt[...] = jnp.transpose(jnp.concatenate(rows, axis=0))

    lane = lax.broadcasted_iota(jnp.int32, (regions, points), 1)
    for b in range(3):
        g = d - 1 + b
        valid = jnp.logical_and(g >= 0, g < n)
        at = pl.ds(pl.multiple_of(jnp.clip(g, 0, n - 1) * regions, regions), regions)
        here = pl.ds(b * regions, regions)
        om = lw_ref[at, :]
        off = li_ref[at, :] - lane
        for o in range(-REACH, REACH + 2):
            c = jnp.where(off == o, om, 0.0) + jnp.where(off == o - 1, 1.0 - om, 0.0)
            coef[o + REACH, here, :] = jnp.where(valid, c, 0.0)
        w = wt[at, :]
        for o in range(2 * REACH + 1):
            wb[o, here, :] = jnp.broadcast_to(w[:, o:o + 1], (regions, points))

    def own(r, _):
        x = e_ref[r]
        x0[regions + r] = x
        eb[r, 0:cols, :] = x.astype(jnp.bfloat16)
        return 0

    lax.fori_loop(0, regions, own, 0)
    zeros = jnp.zeros((cols, points), jnp.float32)

    def clear(first):
        def one(r, _):
            x0[first + r] = zeros
            x2[first + r] = zeros
            return 0
        lax.fori_loop(0, regions, one, 0)

    @pl.when(d == 0)
    def _():
        clear(0)

    @pl.when(d == n - 1)
    def _():
        clear(2 * regions)

    def region(src, dst, r, j, keep):
        m = wb[0, pl.ds(r, 1), :] * src[r - REACH]
        for o in range(1, 2 * REACH + 1):
            m = m + wb[o, pl.ds(r, 1), :] * src[r - REACH + o]
        out = coef[REACH, pl.ds(r, 1), :] * m
        for o in range(-REACH, REACH + 2):
            if o != 0:
                out = out + coef[o + REACH, pl.ds(r, 1), :] * pltpu.roll(
                    m, (-o) % points, 1)
        dst[r] = out
        if keep:
            eb[r - regions, pl.ds(j * cols, cols), :] = out.astype(jnp.bfloat16)

    def advance(src, dst, j, extra):
        def halo_one(i, _):
            region(src, dst, regions - extra + i, j, False)
            region(src, dst, 2 * regions + i, j, False)
            return 0

        def own_one(i, _):
            region(src, dst, regions + i, j, True)
            return 0

        if extra:
            lax.fori_loop(0, extra, halo_one, 0)
        lax.fori_loop(0, regions, own_one, 0)

    def dots(lo, hi):
        tile = min(256, 2 * length)

        def one(i, _):
            r = lax.div(i, 2 * length // tile)
            t = pl.ds(pl.multiple_of(lax.rem(i, 2 * length // tile) * tile, tile), tile)
            p = jnp.dot(eb[r, lo * cols:hi * cols, :], pol[r, :, t],
                        preferred_element_type=jnp.float32)
            acc[lo * cols:hi * cols, t] += p
            return 0

        lax.fori_loop(0, regions * (2 * length // tile), one, 0)

    acc[...] = jnp.zeros_like(acc)
    wait_halo(0)
    bufs = [x0, x1]
    for j in range(1, FIRST):
        advance(bufs[(j - 1) % 2], bufs[j % 2], j, REACH * (FIRST - j))
    advance(bufs[(FIRST - 1) % 2], x2, FIRST, 0)
    start_halo(1)
    policy_copy.wait()
    dots(0, FIRST + 1)
    wait_halo(1)
    src = x2
    for j in range(FIRST + 1, H):
        dst = bufs[j % 2]
        advance(src, dst, j, REACH * (H - 1 - j))
        src = dst
    dots(FIRST + 1, H)

    width = 2 * length
    pos = lax.rem(lax.broadcasted_iota(jnp.int32, (cols, width), 1), length)
    row = lax.broadcasted_iota(jnp.int32, (cols, width), 0)

    def later(x, amount):
        return jnp.where(pos >= amount, pltpu.roll(x, amount, 1), 0.0)

    prev = acc[0:cols, :]
    for j in range(1, H):
        prev = acc[j * cols:(j + 1) * cols, :] + later(prev, 1)
        acc[j * cols:(j + 1) * cols, :] = prev
    step = 1
    while 2 * step < cols:
        moved = pltpu.roll(later(prev, H * step), 2 * step, 0)
        prev = prev + jnp.where(row >= 2 * step, moved, 0.0)
        step *= 2
    carry = jnp.where(row >= 2, pltpu.roll(prev, 2, 0), 0.0)
    for j in range(H):
        v = acc[j * cols:(j + 1) * cols, :] + later(carry, j + 1)
        jp[:, :, j] = v.reshape(chips, 2, 2, width)

    pair = pltpu.make_async_remote_copy(
        src_ref=jp.at[:, 1 - par], dst_ref=ra, send_sem=asem.at[0], recv_sem=asem.at[1],
        device_id={"reg": sib}, device_id_type=pl.DeviceIdType.MESH)
    pair.start()
    pair.wait()

    def part(off):
        q = lax.rem(chip + off, chips)
        return pltpu.make_async_remote_copy(
            src_ref=sb.at[off], dst_ref=rb.at[off],
            send_sem=bsend.at[off], recv_sem=brecv.at[off],
            device_id={"reg": 2 * q + par}, device_id_type=pl.DeviceIdType.MESH)

    for off in range(1, chips):
        q = lax.rem(chip + off, chips)
        sb[off] = jp[q, par] + ra[q]
        part(off).start()
    total = jp[chip, par] + ra[chip]
    for off in range(1, chips):
        part(off).wait()
        total = total + rb[off]
    out_ref[...] = total


def per_device(
    expect_marks, policy_resp, lottery_weight, lottery_index, migration_weight, neighbours
):
    n = lax.axis_size("reg")
    regions, points, marks, outcomes = expect_marks.shape
    shocks, length = policy_resp.shape[2:]
    cols = marks * outcomes
    assert marks == n and outcomes == 2 and shocks == 2 and length == n * H
    assert regions >= REACH * FIRST and regions % 8 == 0
    field = jnp.transpose(expect_marks, (0, 2, 3, 1)).reshape(regions, cols, points)
    policy = policy_resp.reshape(regions, points, shocks * length)
    f32 = jnp.float32
    slab = pltpu.VMEM((3 * regions, cols, points), f32)
    vmem = pl.BlockSpec(memory_space=pltpu.VMEM)
    width = shocks * length
    got = pl.pallas_call(
        functools.partial(kernel, n),
        out_shape=jax.ShapeDtypeStruct((H, outcomes, width), f32),
        in_specs=[vmem, pl.BlockSpec(memory_space=pl.ANY), vmem, vmem, vmem, vmem],
        out_specs=vmem,
        scratch_shapes=[
            slab, slab, slab,
            pltpu.VMEM((regions, H * cols, points), jnp.bfloat16),
            pltpu.VMEM((regions, points, width), jnp.bfloat16),
            pltpu.VMEM((H * cols, width), f32),
            pltpu.VMEM((2 * REACH + 2, 3 * regions, points), f32),
            pltpu.VMEM((2 * REACH + 1, 3 * regions, points), f32),
            pltpu.VMEM((regions * n, 8), f32),
            pltpu.VMEM((n // 2, 2, H, 2, width), f32),
            pltpu.VMEM((n // 2, H, 2, width), f32),
            pltpu.VMEM((n // 2, H, 2, width), f32),
            pltpu.VMEM((n // 2, H, 2, width), f32),
            pltpu.SemaphoreType.DMA,
            pltpu.SemaphoreType.DMA((2, 2)),
            pltpu.SemaphoreType.DMA((2, 2)),
            pltpu.SemaphoreType.DMA((2,)),
            pltpu.SemaphoreType.DMA((n // 2,)),
            pltpu.SemaphoreType.DMA((n // 2,)),
        ],
        compiler_params=pltpu.CompilerParams(
            collective_id=0, has_side_effects=True, vmem_limit_bytes=56 * 2**20),
        name="jacobian",
    )(field, policy, lottery_weight, lottery_index,
      jnp.transpose(migration_weight), jnp.transpose(neighbours))
    return got.reshape(H, outcomes, shocks, length)


def solution(mesh):
    return jax.shard_map(
        per_device,
        mesh=mesh,
        in_specs=(
            P(("grp", "reg"), None, None, None),
            P(("grp", "reg"), None, None, None),
            P("grp", None),
            P("grp", None),
            P("grp", None),
            P("grp", None),
        ),
        out_specs=P(("grp", "reg"), None, None, None),
        check_vma=False,
    )
```

```python
import functools
import jax
import jax.numpy as jnp
from jax import lax
from jax.experimental import pallas as pl
from jax.experimental.pallas import tpu as pltpu
from jax.sharding import PartitionSpec as P

REACH = 2
H = 8
FIRST = 4


def kernel(n, e_hbm, pol_hbm, lw_hbm, li_hbm, mw_hbm, nb_hbm, out_ref,
           x0, x1, x2, x3, x4, ebuf, pbuf, pf, lwb, lib, mwb, nbb,
           eb, pol, acc, coef, wb, wt, jp, ra, sb, rb,
           isem, hsend, hrecv, asem, bsend, brecv):
    regions, marks, _, points = ebuf.shape
    cols = 2 * marks
    length = pol.shape[2] // 2
    chips = n // 2
    d = lax.axis_index("reg")
    par = lax.rem(d, 2)
    chip = lax.div(d, 2)
    sib = d + 1 - 2 * par

    barrier = pltpu.get_barrier_semaphore()

    def greet(other):
        pl.semaphore_signal(barrier, inc=1, device_id={"reg": other},
                            device_id_type=pl.DeviceIdType.MESH)

    @pl.when(d > 0)
    def _():
        greet(d - 1)

    @pl.when(d < n - 1)
    def _():
        greet(d + 1)

    for off in range(1, chips):
        greet(2 * lax.rem(chip + off, chips) + par)

    def table_rows(b):
        g = jnp.clip(d - 1 + b, 0, n - 1) * regions
        return pl.ds(pl.multiple_of(g, regions), regions)

    loads = [(e_hbm, ebuf), (mw_hbm, mwb), (nb_hbm, nbb)]
    for b in range(3):
        here = pl.ds(b * regions, regions)
        loads.append((lw_hbm.at[table_rows(b)], lwb.at[here]))
        loads.append((li_hbm.at[table_rows(b)], lib.at[here]))
    loads.append((pol_hbm, pbuf))
    loads = [pltpu.make_async_copy(a, v, isem.at[q]) for q, (a, v) in enumerate(loads)]
    for c in loads:
        c.start()

    loads[0].wait()

    def own(r, _):
        x = ebuf[r].reshape(cols, points)
        x0[regions + r] = x
        eb[r, 0:cols, :] = x.astype(jnp.bfloat16)
        return 0

    lax.fori_loop(0, regions, own, 0)

    for c in loads[1:-1]:
        c.wait()
    mw = mwb[...]
    mix = mw / jnp.sum(mw, axis=0, keepdims=True)
    offs = nbb[...] - lax.broadcasted_iota(jnp.int32, mw.shape, 1)
    rows = [jnp.sum(jnp.where(offs == o, mix, 0.0), axis=0, keepdims=True)
            for o in range(-REACH, REACH + 1)]
    rows.append(jnp.zeros((8 - len(rows), mw.shape[1]), jnp.float32))
    wt[...] = jnp.transpose(jnp.concatenate(rows, axis=0))

    lane = lax.broadcasted_iota(jnp.int32, (regions, points), 1)
    for b in range(3):
        g = d - 1 + b
        valid = jnp.logical_and(g >= 0, g < n)
        here = pl.ds(b * regions, regions)
        om = lwb[here, :]
        off = lib[here, :] - lane
        for o in range(-REACH, REACH + 2):
            c = jnp.where(off == o, om, 0.0) + jnp.where(off == o - 1, 1.0 - om, 0.0)
            coef[o + REACH, here, :] = jnp.where(valid, c, 0.0)
        w = wt[table_rows(b), :]
        for o in range(2 * REACH + 1):
            wb[o, here, :] = jnp.broadcast_to(w[:, o:o + 1], (regions, points))

    zeros = jnp.zeros((cols, points), jnp.float32)

    def clear(first):
        def one(r, _):
            x0[first + r] = zeros
            x4[first + r] = zeros
            return 0
        lax.fori_loop(0, regions, one, 0)

    @pl.when(d == 0)
    def _():
        clear(0)

    @pl.when(d == n - 1)
    def _():
        clear(2 * regions)

    ends = jnp.where(d > 0, 1, 0) + jnp.where(d < n - 1, 1, 0)
    pl.semaphore_wait(barrier, ends + (chips - 1))

    def halo(stage, to_left, c):
        buf = x4 if stage else x0
        near = c * REACH
        if to_left:
            src, dst = regions + near, 2 * regions + near
        else:
            src, dst = 2 * regions - near - REACH, regions - near - REACH
        side = 0 if to_left else 1
        return pltpu.make_async_remote_copy(
            src_ref=buf.at[pl.ds(src, REACH)], dst_ref=buf.at[pl.ds(dst, REACH)],
            send_sem=hsend.at[stage, side, c], recv_sem=hrecv.at[stage, side, c],
            device_id={"reg": d - 1 if to_left else d + 1},
            device_id_type=pl.DeviceIdType.MESH)

    def start_halo(stage, chunks):
        @pl.when(d > 0)
        def _():
            for c in chunks:
                halo(stage, True, c).start()

        @pl.when(d < n - 1)
        def _():
            for c in chunks:
                halo(stage, False, c).start()

    def wait_halo(stage, c):
        @pl.when(d > 0)
        def _():
            halo(stage, False, c).wait_recv()

        @pl.when(d < n - 1)
        def _():
            halo(stage, True, c).wait_recv()

    def sent_halo(stage, chunks):
        @pl.when(d > 0)
        def _():
            for c in chunks:
                halo(stage, True, c).wait_send()

        @pl.when(d < n - 1)
        def _():
            for c in chunks:
                halo(stage, False, c).wait_send()

    chunks0 = range(FIRST)
    chunks1 = range(H - 1 - FIRST)
    start_halo(0, chunks0)

    loads[-1].wait()

    def split_shocks(r, _):
        v = pbuf[pl.ds(pl.multiple_of(r * 2 * points, 2 * points), 2 * points), :]
        v = v.astype(jnp.float32)
        for t in range(length // 128):
            pf[t] = v[:, t * 128:(t + 1) * 128]
        for t in range(length // 128):
            for i in range(2):
                at = i * length + t * 128
                pol[r, :, at:at + 128] = pf[t, pl.ds(i, points, stride=2), :].astype(
                    jnp.bfloat16)
        return 0

    lax.fori_loop(0, regions, split_shocks, 0)

    def piece(src, dst, r, j, keep, sl):
        m = wb[0, pl.ds(r, 1), :] * src[r - REACH, sl, :]
        for o in range(1, 2 * REACH + 1):
            m = m + wb[o, pl.ds(r, 1), :] * src[r - REACH + o, sl, :]
        out = coef[REACH, pl.ds(r, 1), :] * m
        for o in range(-REACH, REACH + 2):
            if o != 0:
                out = out + coef[o + REACH, pl.ds(r, 1), :] * pltpu.roll(
                    m, (-o) % points, 1)
        dst[r, sl, :] = out
        if keep:
            return out.astype(jnp.bfloat16)

    def several(src, dst, which, j, keep):
        def block(i, _):
            c0 = pl.multiple_of(i * 32, 32)
            for r in which:
                kept = piece(src, dst, r, j, keep, pl.ds(c0, 32))
                if keep:
                    eb[r - regions, pl.ds(j * cols + c0, 32), :] = kept
            return 0

        if cols == 32:
            block(0, 0)
        else:
            lax.fori_loop(0, cols // 32, block, 0)

    def ring(src, dst, c, j):
        near = c * REACH
        lo, hi = regions - near - REACH, 2 * regions + near
        several(src, dst, [lo + q for q in range(REACH)] + [hi + q for q in range(REACH)],
                j, False)

    def inner(src, dst, j, start=0):
        def one(i, _):
            several(src, dst, [regions + start + 4 * i + q for q in range(4)], j, True)
            return 0
        lax.fori_loop(0, (regions - 2 * start) // 4, one, 0)

    def edge(src, dst, j):
        several(src, dst, [regions, regions + 1, 2 * regions - 2, 2 * regions - 1], j, True)

    def dots(lo, hi):
        tile = min(256, 2 * length)

        def one(i, _):
            r = lax.div(i, 2 * length // tile)
            t = pl.ds(pl.multiple_of(lax.rem(i, 2 * length // tile) * tile, tile), tile)
            p = jnp.dot(eb[r, lo * cols:hi * cols, :], pol[r, :, t],
                        preferred_element_type=jnp.float32)
            acc[lo * cols:hi * cols, t] += p
            return 0

        lax.fori_loop(0, regions * (2 * length // tile), one, 0)

    acc[...] = jnp.zeros_like(acc)
    first = [x0, x1, x2, x3, x4]
    for c in chunks0:
        wait_halo(0, c)
        for j in range(1, c + 1):
            ring(first[j - 1], first[j], c - j, j)
        if c + 1 < FIRST:
            inner(first[c], first[c + 1], c + 1)
        else:
            edge(first[c], first[c + 1], c + 1)
            start_halo(1, [0])
            inner(first[c], first[c + 1], c + 1, REACH)
            start_halo(1, chunks1[1:])
    dots(0, FIRST + 1)
    second = [x4, x1, x2, x3]
    for c in chunks1:
        wait_halo(1, c)
        for j in range(1, c + 1):
            ring(second[j - 1], second[j], c - j, FIRST + j)
        inner(second[c], second[c + 1], FIRST + c + 1)
    dots(FIRST + 1, H)
    sent_halo(0, chunks0)
    sent_halo(1, chunks1)

    width = 2 * length
    pos = lax.rem(lax.broadcasted_iota(jnp.int32, (cols, width), 1), length)
    row = lax.broadcasted_iota(jnp.int32, (cols, width), 0)

    def later(x, amount):
        return jnp.where(pos >= amount, pltpu.roll(x, amount, 1), 0.0)

    prev = acc[0:cols, :]
    for j in range(1, H):
        prev = acc[j * cols:(j + 1) * cols, :] + later(prev, 1)
        acc[j * cols:(j + 1) * cols, :] = prev
    step = 1
    while 2 * step < cols:
        moved = pltpu.roll(later(prev, H * step), 2 * step, 0)
        prev = prev + jnp.where(row >= 2 * step, moved, 0.0)
        step *= 2
    carry = jnp.where(row >= 2, pltpu.roll(prev, 2, 0), 0.0)
    for j in range(H):
        v = acc[j * cols:(j + 1) * cols, :] + later(carry, j + 1)
        jp[:, :, j] = v.reshape(chips, 2, 2, width)

    pair = pltpu.make_async_remote_copy(
        src_ref=jp.at[:, 1 - par], dst_ref=ra, send_sem=asem.at[0], recv_sem=asem.at[1],
        device_id={"reg": sib}, device_id_type=pl.DeviceIdType.MESH)
    pair.start()
    pair.wait()

    def part(off):
        q = lax.rem(chip + off, chips)
        return pltpu.make_async_remote_copy(
            src_ref=sb.at[off], dst_ref=rb.at[off],
            send_sem=bsend.at[off], recv_sem=brecv.at[off],
            device_id={"reg": 2 * q + par}, device_id_type=pl.DeviceIdType.MESH)

    for off in range(1, chips):
        q = lax.rem(chip + off, chips)
        sb[off] = jp[q, par] + ra[q]
        part(off).start()
    total = jp[chip, par] + ra[chip]
    for off in range(1, chips):
        part(off).wait()
        total = total + rb[off]
    for i in range(2):
        out_ref[:, :, i, :] = total[:, :, i * length:(i + 1) * length]


def per_device(
    expect_marks, policy_resp, lottery_weight, lottery_index, migration_weight, neighbours
):
    n = lax.axis_size("reg")
    regions, points, marks, outcomes = expect_marks.shape
    shocks, length = policy_resp.shape[2:]
    cols = marks * outcomes
    assert marks == n and outcomes == 2 and shocks == 2 and length == n * H
    assert regions >= REACH * FIRST and regions % 8 == 0
    field = jnp.transpose(expect_marks, (0, 2, 3, 1))
    policy = policy_resp.reshape(regions * points * shocks, length)
    f32 = jnp.float32
    slab = pltpu.VMEM((3 * regions, cols, points), f32)
    width = shocks * length
    entries = neighbours.shape[1]
    return pl.pallas_call(
        functools.partial(kernel, n),
        out_shape=jax.ShapeDtypeStruct((H, outcomes, shocks, length), f32),
        in_specs=[pl.BlockSpec(memory_space=pl.ANY)] * 6,
        out_specs=pl.BlockSpec(memory_space=pltpu.VMEM),
        scratch_shapes=[
            slab, slab, slab, slab, slab,
            pltpu.VMEM((regions, marks, outcomes, points), f32),
            pltpu.VMEM((regions * points * shocks, length), jnp.bfloat16),
            pltpu.VMEM((length // 128, shocks * points, 128), f32),
            pltpu.VMEM((3 * regions, points), f32),
            pltpu.VMEM((3 * regions, points), jnp.int32),
            pltpu.VMEM((entries, regions * n), f32),
            pltpu.VMEM((entries, regions * n), jnp.int32),
            pltpu.VMEM((regions, H * cols, points), jnp.bfloat16),
            pltpu.VMEM((regions, points, width), jnp.bfloat16),
            pltpu.VMEM((H * cols, width), f32),
            pltpu.VMEM((2 * REACH + 2, 3 * regions, points), f32),
            pltpu.VMEM((2 * REACH + 1, 3 * regions, points), f32),
            pltpu.VMEM((regions * n, 8), f32),
            pltpu.VMEM((n // 2, 2, H, 2, width), f32),
            pltpu.VMEM((n // 2, H, 2, width), f32),
            pltpu.VMEM((n // 2, H, 2, width), f32),
            pltpu.VMEM((n // 2, H, 2, width), f32),
            pltpu.SemaphoreType.DMA((10,)),
            pltpu.SemaphoreType.DMA((2, 2, FIRST)),
            pltpu.SemaphoreType.DMA((2, 2, FIRST)),
            pltpu.SemaphoreType.DMA((2,)),
            pltpu.SemaphoreType.DMA((n // 2,)),
            pltpu.SemaphoreType.DMA((n // 2,)),
        ],
        compiler_params=pltpu.CompilerParams(
            collective_id=0, has_side_effects=True, vmem_limit_bytes=56 * 2**20),
        name="jacobian",
    )(field, policy, lottery_weight, lottery_index,
      jnp.transpose(migration_weight), jnp.transpose(neighbours))


def solution(mesh):
    return jax.shard_map(
        per_device,
        mesh=mesh,
        in_specs=(
            P(("grp", "reg"), None, None, None),
            P(("grp", "reg"), None, None, None),
            P("grp", None),
            P("grp", None),
            P("grp", None),
            P("grp", None),
        ),
        out_specs=P(("grp", "reg"), None, None, None),
        check_vma=False,
    )
```

```python
import functools
import jax
import jax.numpy as jnp
from jax import lax
from jax.experimental import pallas as pl
from jax.experimental.pallas import tpu as pltpu
from jax.sharding import PartitionSpec as P

REACH = 2
H = 8
FIRST = 4


def kernel(n, e_hbm, pol_hbm, lw_hbm, li_hbm, mw_hbm, nb_hbm, out_ref,
           x0, x1, x2, x3, x4, ebuf, pbuf, pf, lwb, lib, mwb, nbb,
           eb, pol, acc, coef, wb, wt, jp, ra, sb, rb,
           isem, hsend, hrecv, asem, bsend, brecv):
    regions, marks, _, points = ebuf.shape
    cols = 2 * marks
    length = pol.shape[2] // 2
    chips = n // 2
    d = lax.axis_index("reg")
    par = lax.rem(d, 2)
    chip = lax.div(d, 2)
    sib = d + 1 - 2 * par

    barrier = pltpu.get_barrier_semaphore()

    def greet(other):
        pl.semaphore_signal(barrier, inc=1, device_id={"reg": other},
                            device_id_type=pl.DeviceIdType.MESH)

    @pl.when(d > 0)
    def _():
        greet(d - 1)

    @pl.when(d < n - 1)
    def _():
        greet(d + 1)

    def table_rows(b):
        g = jnp.clip(d - 1 + b, 0, n - 1) * regions
        return pl.ds(pl.multiple_of(g, regions), regions)

    loads = [(e_hbm, ebuf), (mw_hbm, mwb), (nb_hbm, nbb)]
    for b in range(3):
        here = pl.ds(b * regions, regions)
        loads.append((lw_hbm.at[table_rows(b)], lwb.at[here]))
        loads.append((li_hbm.at[table_rows(b)], lib.at[here]))
    loads.append((pol_hbm, pbuf))
    loads = [pltpu.make_async_copy(a, v, isem.at[q]) for q, (a, v) in enumerate(loads)]
    for c in loads:
        c.start()

    for off in range(1, chips):
        greet(2 * lax.rem(chip + off, chips) + par)

    loads[0].wait()

    def own(r, _):
        x = ebuf[r].reshape(cols, points)
        x0[regions + r] = x
        eb[r, 0:cols, :] = x.astype(jnp.bfloat16)
        return 0

    lax.fori_loop(0, regions, own, 0)

    ends = jnp.where(d > 0, 1, 0) + jnp.where(d < n - 1, 1, 0)
    pl.semaphore_wait(barrier, ends + (chips - 1))

    def halo(stage, to_left, c, part):
        some = pl.ds(part * (cols // 2), cols // 2)
        buf = x4 if stage else x0
        near = c * REACH
        if to_left:
            src, dst = regions + near, 2 * regions + near
        else:
            src, dst = 2 * regions - near - REACH, regions - near - REACH
        side = 0 if to_left else 1
        return pltpu.make_async_remote_copy(
            src_ref=buf.at[pl.ds(src, REACH), some], dst_ref=buf.at[pl.ds(dst, REACH), some],
            send_sem=hsend.at[stage, side, c, part],
            recv_sem=hrecv.at[stage, side, c, part],
            device_id={"reg": d - 1 if to_left else d + 1},
            device_id_type=pl.DeviceIdType.MESH)

    def start_halo(stage, chunks, part):
        @pl.when(d > 0)
        def _():
            for c in chunks:
                halo(stage, True, c, part).start()

        @pl.when(d < n - 1)
        def _():
            for c in chunks:
                halo(stage, False, c, part).start()

    def wait_halo(stage, c, part):
        @pl.when(d > 0)
        def _():
            halo(stage, False, c, part).wait_recv()

        @pl.when(d < n - 1)
        def _():
            halo(stage, True, c, part).wait_recv()

    def sent_halo(stage, chunks, part):
        @pl.when(d > 0)
        def _():
            for c in chunks:
                halo(stage, True, c, part).wait_send()

        @pl.when(d < n - 1)
        def _():
            for c in chunks:
                halo(stage, False, c, part).wait_send()

    chunks0 = range(FIRST)
    chunks1 = range(H - 1 - FIRST)
    start_halo(0, chunks0, 0)
    start_halo(0, chunks0, 1)

    for c in loads[1:-1]:
        c.wait()
    mw = mwb[...]
    mix = mw / jnp.sum(mw, axis=0, keepdims=True)
    offs = nbb[...] - lax.broadcasted_iota(jnp.int32, mw.shape, 1)
    rows = [jnp.sum(jnp.where(offs == o, mix, 0.0), axis=0, keepdims=True)
            for o in range(-REACH, REACH + 1)]
    rows.append(jnp.zeros((8 - len(rows), mw.shape[1]), jnp.float32))
    wt[...] = jnp.transpose(jnp.concatenate(rows, axis=0))

    lane = lax.broadcasted_iota(jnp.int32, (regions, points), 1)
    for b in range(3):
        g = d - 1 + b
        valid = jnp.logical_and(g >= 0, g < n)
        here = pl.ds(b * regions, regions)
        om = lwb[here, :]
        off = lib[here, :] - lane
        for o in range(-REACH, REACH + 2):
            c = jnp.where(off == o, om, 0.0) + jnp.where(off == o - 1, 1.0 - om, 0.0)
            coef[o + REACH, here, :] = jnp.where(valid, c, 0.0)
        w = wt[table_rows(b), :]
        for o in range(2 * REACH + 1):
            wb[o, here, :] = jnp.broadcast_to(w[:, o:o + 1], (regions, points))

    zeros = jnp.zeros((cols, points), jnp.float32)

    def clear(first):
        def one(r, _):
            x0[first + r] = zeros
            x4[first + r] = zeros
            return 0
        lax.fori_loop(0, regions, one, 0)

    @pl.when(d == 0)
    def _():
        clear(0)

    @pl.when(d == n - 1)
    def _():
        clear(2 * regions)

    loads[-1].wait()

    def split_shocks(r, _):
        v = pbuf[pl.ds(pl.multiple_of(r * 2 * points, 2 * points), 2 * points), :]
        v = v.astype(jnp.float32)
        for t in range(length // 128):
            pf[t] = v[:, t * 128:(t + 1) * 128]
        for t in range(length // 128):
            for i in range(2):
                at = i * length + t * 128
                pol[r, :, at:at + 128] = pf[t, pl.ds(i, points, stride=2), :].astype(
                    jnp.bfloat16)
        return 0

    lax.fori_loop(0, regions, split_shocks, 0)

    def piece(src, dst, r, j, keep, sl):
        m = wb[0, pl.ds(r, 1), :] * src[r - REACH, sl, :]
        for o in range(1, 2 * REACH + 1):
            m = m + wb[o, pl.ds(r, 1), :] * src[r - REACH + o, sl, :]
        out = coef[REACH, pl.ds(r, 1), :] * m
        for o in range(-REACH, REACH + 2):
            if o != 0:
                out = out + coef[o + REACH, pl.ds(r, 1), :] * pltpu.roll(
                    m, (-o) % points, 1)
        dst[r, sl, :] = out
        if keep:
            return out.astype(jnp.bfloat16)

    half = cols // 2

    def several(src, dst, which, j, keep, part):
        def block(i, _):
            c0 = part * half + i * 16
            if half != 16:
                c0 = pl.multiple_of(c0, 16)
            for r in which:
                kept = piece(src, dst, r, j, keep, pl.ds(c0, 16))
                if keep:
                    eb[r - regions, pl.ds(j * cols + c0, 16), :] = kept
            return 0

        if half == 16:
            block(0, 0)
        else:
            lax.fori_loop(0, half // 16, block, 0)

    def ring(src, dst, c, j, part):
        near = c * REACH
        lo, hi = regions - near - REACH, 2 * regions + near
        several(src, dst, [lo + q for q in range(REACH)] + [hi + q for q in range(REACH)],
                j, False, part)

    def inner(src, dst, j, part, start=0):
        def one(i, _):
            several(src, dst, [regions + start + 4 * i + q for q in range(4)], j, True, part)
            return 0
        lax.fori_loop(0, (regions - 2 * start) // 4, one, 0)

    def edge(src, dst, j, part):
        several(src, dst, [regions, regions + 1, 2 * regions - 2, 2 * regions - 1],
                j, True, part)

    def dots(lo, hi):
        tile = min(256, 2 * length)

        def one(i, _):
            r = lax.div(i, 2 * length // tile)
            t = pl.ds(pl.multiple_of(lax.rem(i, 2 * length // tile) * tile, tile), tile)
            p = jnp.dot(eb[r, lo * cols:hi * cols, :], pol[r, :, t],
                        preferred_element_type=jnp.float32)
            acc[lo * cols:hi * cols, t] += p
            return 0

        lax.fori_loop(0, regions * (2 * length // tile), one, 0)

    acc[...] = jnp.zeros_like(acc)
    first = [x0, x1, x2, x3, x4]
    for part in range(2):
        for c in chunks0:
            wait_halo(0, c, part)
            for j in range(1, c + 1):
                ring(first[j - 1], first[j], c - j, j, part)
            if c + 1 < FIRST:
                inner(first[c], first[c + 1], c + 1, part)
            else:
                edge(first[c], first[c + 1], c + 1, part)
                start_halo(1, [0], part)
                inner(first[c], first[c + 1], c + 1, part, REACH)
                start_halo(1, chunks1[1:], part)
    dots(0, FIRST + 1)
    second = [x4, x1, x2, x3]
    for part in range(2):
        for c in chunks1:
            wait_halo(1, c, part)
            for j in range(1, c + 1):
                ring(second[j - 1], second[j], c - j, FIRST + j, part)
            inner(second[c], second[c + 1], FIRST + c + 1, part)
    dots(FIRST + 1, H)
    for part in range(2):
        sent_halo(0, chunks0, part)
        sent_halo(1, chunks1, part)

    width = 2 * length
    pos = lax.rem(lax.broadcasted_iota(jnp.int32, (cols, width), 1), length)
    row = lax.broadcasted_iota(jnp.int32, (cols, width), 0)

    def later(x, amount):
        return jnp.where(pos >= amount, pltpu.roll(x, amount, 1), 0.0)

    prev = acc[0:cols, :]
    for j in range(1, H):
        prev = acc[j * cols:(j + 1) * cols, :] + later(prev, 1)
        acc[j * cols:(j + 1) * cols, :] = prev
    step = 1
    while 2 * step < cols:
        moved = pltpu.roll(later(prev, H * step), 2 * step, 0)
        prev = prev + jnp.where(row >= 2 * step, moved, 0.0)
        step *= 2
    carry = jnp.where(row >= 2, pltpu.roll(prev, 2, 0), 0.0)
    for j in range(H):
        v = acc[j * cols:(j + 1) * cols, :] + later(carry, j + 1)
        jp[:, :, j] = v.reshape(chips, 2, 2, width)

    pair = pltpu.make_async_remote_copy(
        src_ref=jp.at[:, 1 - par], dst_ref=ra, send_sem=asem.at[0], recv_sem=asem.at[1],
        device_id={"reg": sib}, device_id_type=pl.DeviceIdType.MESH)
    pair.start()
    pair.wait()

    def part(off):
        q = lax.rem(chip + off, chips)
        return pltpu.make_async_remote_copy(
            src_ref=sb.at[off], dst_ref=rb.at[off],
            send_sem=bsend.at[off], recv_sem=brecv.at[off],
            device_id={"reg": 2 * q + par}, device_id_type=pl.DeviceIdType.MESH)

    for off in range(1, chips):
        q = lax.rem(chip + off, chips)
        sb[off] = jp[q, par] + ra[q]
        part(off).start()
    total = jp[chip, par] + ra[chip]
    for off in range(1, chips):
        part(off).wait()
        total = total + rb[off]
    for i in range(2):
        out_ref[:, :, i, :] = total[:, :, i * length:(i + 1) * length]


def per_device(
    expect_marks, policy_resp, lottery_weight, lottery_index, migration_weight, neighbours
):
    n = lax.axis_size("reg")
    regions, points, marks, outcomes = expect_marks.shape
    shocks, length = policy_resp.shape[2:]
    cols = marks * outcomes
    assert marks == n and outcomes == 2 and shocks == 2 and length == n * H
    assert regions >= REACH * FIRST and regions % 8 == 0
    field = jnp.transpose(expect_marks, (0, 2, 3, 1))
    policy = policy_resp.reshape(regions * points * shocks, length)
    f32 = jnp.float32
    slab = pltpu.VMEM((3 * regions, cols, points), f32)
    width = shocks * length
    entries = neighbours.shape[1]
    return pl.pallas_call(
        functools.partial(kernel, n),
        out_shape=jax.ShapeDtypeStruct((H, outcomes, shocks, length), f32),
        in_specs=[pl.BlockSpec(memory_space=pl.ANY)] * 6,
        out_specs=pl.BlockSpec(memory_space=pltpu.VMEM),
        scratch_shapes=[
            slab, slab, slab, slab, slab,
            pltpu.VMEM((regions, marks, outcomes, points), f32),
            pltpu.VMEM((regions * points * shocks, length), jnp.bfloat16),
            pltpu.VMEM((length // 128, shocks * points, 128), f32),
            pltpu.VMEM((3 * regions, points), f32),
            pltpu.VMEM((3 * regions, points), jnp.int32),
            pltpu.VMEM((entries, regions * n), f32),
            pltpu.VMEM((entries, regions * n), jnp.int32),
            pltpu.VMEM((regions, H * cols, points), jnp.bfloat16),
            pltpu.VMEM((regions, points, width), jnp.bfloat16),
            pltpu.VMEM((H * cols, width), f32),
            pltpu.VMEM((2 * REACH + 2, 3 * regions, points), f32),
            pltpu.VMEM((2 * REACH + 1, 3 * regions, points), f32),
            pltpu.VMEM((regions * n, 8), f32),
            pltpu.VMEM((n // 2, 2, H, 2, width), f32),
            pltpu.VMEM((n // 2, H, 2, width), f32),
            pltpu.VMEM((n // 2, H, 2, width), f32),
            pltpu.VMEM((n // 2, H, 2, width), f32),
            pltpu.SemaphoreType.DMA((10,)),
            pltpu.SemaphoreType.DMA((2, 2, FIRST, 2)),
            pltpu.SemaphoreType.DMA((2, 2, FIRST, 2)),
            pltpu.SemaphoreType.DMA((2,)),
            pltpu.SemaphoreType.DMA((n // 2,)),
            pltpu.SemaphoreType.DMA((n // 2,)),
        ],
        compiler_params=pltpu.CompilerParams(
            collective_id=0, has_side_effects=True, vmem_limit_bytes=56 * 2**20),
        name="jacobian",
    )(field, policy, lottery_weight, lottery_index,
      jnp.transpose(migration_weight), jnp.transpose(neighbours))


def solution(mesh):
    return jax.shard_map(
        per_device,
        mesh=mesh,
        in_specs=(
            P(("grp", "reg"), None, None, None),
            P(("grp", "reg"), None, None, None),
            P("grp", None),
            P("grp", None),
            P("grp", None),
            P("grp", None),
        ),
        out_specs=P(("grp", "reg"), None, None, None),
        check_vma=False,
    )
```
